32 devices in a mesh: rep: 8 (over y, x, core), tp: 4 (over z).
Axes of the slice: x: 2, y: 2, z: 4, core: 2. Of those that a mesh axis runs over, the one named last changes fastest.
Arguments:
- tokens: bfloat16 [128, 1024], P('rep'), may hold values from -6 to 6
- lengths: int32 [128], P('rep'), may hold values from 1 to 256, as said below
- prompt_group: int32 [128], P('rep'), may hold values from 0 to 7
- span_close: int32 [128], P('rep'), may hold values 0 or 1
- out_slot: int32 [8, 2], P('rep'), may hold values from 0 to 15, as said below
- move_dest: int32 [8, 2], P('rep'), may hold values from 0 to 7, as said below
- page_table: int32 [128, 2, 1], P('rep'), may hold values from 0 to 15, as said below
- cache_pool: bfloat16 [128, 16, 128, 256], P('rep', 'tp'), may hold values from -6 to 6
- prefix_cache: bfloat16 [8, 16, 64, 256], P(None, 'tp'), may hold values from -6 to 6
- memory: float32 [128, 16, 64, 128], P('rep', 'tp'), may hold values from -2 to 2
- norm_attn: float32 [1024], replicated, may hold values from 0.5 to 1.5
- norm_mlp: float32 [1024], replicated, may hold values from 0.5 to 1.5
- qkv_weight: bfloat16 [1024, 3072], P(None, 'tp'), may hold values from -0.1875 to 0.1875
- out_weight: bfloat16 [1024, 1024], P('tp'), may hold values from -0.1875 to 0.1875
- gate_weight: bfloat16 [1024, 2816], P(None, 'tp'), may hold values from -0.1875 to 0.1875
- up_weight: bfloat16 [1024, 2816], P(None, 'tp'), may hold values from -0.1875 to 0.1875
- down_weight: bfloat16 [2816, 1024], P('tp'), may hold values from -0.109375 to 0.109375
- forget: float32 [8], replicated, may hold values from 0.5 to 0.99
- write_rate: float32 [8], replicated, may hold values from 0.1 to 0.9
Outputs:
- out_rows: bfloat16 [128, 1024], P('rep')
- new_memory: float32 [128, 16, 64, 128], P('rep', 'tp')
- new_cache_pool: bfloat16 [128, 16, 128, 256], P('rep', 'tp')
The draws below stay inside these ranges and needn't reach their ends.
Inputs may be any that keep to these rules, and one draw needn't show every extreme that they name: `lengths`: the cached tokens of a request; some request of every replica holds 256. `out_slot`: the 2 slots of one replica are distinct. For each m, move_dest[:, m] is a permutation of the replicas. `page_table`: for each replica and half, the entries of its 16 slots are a permutation of 0 to 15.
All inputs are finite; a program needn't handle non-finite values. No bound on the sum of `span_close` on one device may be relied on, other than what follows from the above.
Results may differ from the reference program's by a relative error of at most 0.013.
Values may be sent and summed in bfloat16 or wider, within the bound.
A program may use at most 64 MiB of HBM per device.

```python
import jax
import jax.numpy as jnp
from jax import lax

D = 1024
HEADS = 8
HEAD = 128
FF = 2816
PAGE = 128
HP = 1
PREFIX = 128
GROUPS = 8
MOVES = 2
REQ_DEV = 16
REQUESTS = 128
POOL = 16
SECTIONS = 16
N_REP = 8


def draw_lengths(key, part):
    values = jax.random.randint(key, (REQUESTS,), 1, 2 * HP * PAGE + 1)
    return values.at[::REQ_DEV].set(2 * HP * PAGE).astype(jnp.int32)


def draw_out_slot(key, part):
    keys = jax.random.split(key, N_REP)
    rows = jax.vmap(lambda single: jax.random.permutation(single, REQ_DEV)[:MOVES])(keys)
    return rows.astype(jnp.int32)


def draw_move_dest(key, part):
    keys = jax.random.split(key, MOVES)
    columns = jax.vmap(lambda single: jax.random.permutation(single, N_REP))(keys)
    return columns.T.astype(jnp.int32)


def draw_page_table(key, part):
    keys = jax.random.split(key, N_REP * 2)
    perms = jax.vmap(lambda single: jax.random.permutation(single, REQ_DEV * HP))(keys)
    perms = perms.reshape(N_REP, 2, REQ_DEV, HP).transpose(0, 2, 1, 3)
    return perms.reshape(REQUESTS, 2, HP).astype(jnp.int32)


def touch_ends(drawn, stream_key, smallest, largest):
    longest = drawn.shape.index(max(drawn.shape))
    spots = []
    for shift in (0, 1):
        where = [jax.random.randint(jax.random.fold_in(stream_key, axis), (), 0, length) for axis, length in enumerate(drawn.shape)]
        where[longest] = (where[longest] + shift) % drawn.shape[longest]
        spots.append(tuple(where))
    return drawn.at[spots[0]].set(smallest).at[spots[1]].set(largest)


def block_scale(rng, extent, pieces, least, high):
    loudness = 1.0
    for axis_at, shards_of in pieces:
        draws = jax.random.uniform(jax.random.fold_in(jax.random.fold_in(rng, 6), axis_at), (shards_of,), jnp.float32, least / len(pieces), high / len(pieces))
        loudness = loudness * jnp.repeat(jnp.exp(draws), extent[axis_at] // shards_of).reshape((-1,) + (1,) * (len(extent) - 1 - axis_at))
    return loudness


def scatter_about(own_key, dims, width, bound, cuts=(), dtype=jnp.bfloat16):
    gain = block_scale(own_key, dims, cuts, -0.22, 0.18) if cuts else 1.0
    values = jax.random.normal(own_key, dims, jnp.float32) * width * gain
    return jnp.minimum(jnp.maximum(values, -bound), bound).astype(dtype)


def setup_inputs(seed: int = 0) -> dict:
    splits = jax.random.split(jax.random.key(seed), 20)
    tokens = scatter_about(splits[0], (REQUESTS, D), 1.0, 6.0, ((0, 8),))
    lengths = draw_lengths(jax.random.fold_in(splits[19], 71), 0)
    prompt_group = touch_ends(jax.random.randint(splits[2], (REQUESTS,), 0, GROUPS), jax.random.fold_in(splits[2], 1), 0, GROUPS - 1).astype(jnp.int32)
    span_close = touch_ends((jax.random.randint(splits[3], (REQUESTS,), 0, 2) < 1).astype(jnp.int32), jax.random.fold_in(splits[3], 1), 0, 1)
    out_slot = draw_out_slot(jax.random.fold_in(splits[19], 71), 0)
    move_dest = draw_move_dest(jax.random.fold_in(splits[19], 71), 0)
    page_table = draw_page_table(jax.random.fold_in(splits[19], 71), 0)
    cache_pool = scatter_about(splits[7], (N_REP * POOL, SECTIONS, PAGE, 2 * HEAD), 1.0, 6.0, ((0, 8), (1, 4)))
    prefix_cache = scatter_about(splits[8], (GROUPS, SECTIONS, PREFIX // 2, 2 * HEAD), 1.0, 6.0, ((1, 4),))
    memory = scatter_about(splits[9], (REQUESTS, SECTIONS, HEAD // 2, HEAD), 0.3, 2.0, ((0, 8), (1, 4)), jnp.float32)
    norm_attn = jnp.clip(1.0 + 0.1 * jax.random.normal(splits[10], (D,), jnp.float32), 0.5, 1.5)
    norm_mlp = jnp.clip(1.0 + 0.1 * jax.random.normal(splits[11], (D,), jnp.float32), 0.5, 1.5)
    qkv_weight = scatter_about(splits[12], (D, 3 * D), D ** -0.5, 0.1875, ((1, 4),))
    out_weight = scatter_about(splits[13], (D, D), D ** -0.5, 0.1875, ((0, 4),))
    gate_weight = scatter_about(splits[14], (D, FF), D ** -0.5, 0.1875, ((1, 4),))
    up_weight = scatter_about(splits[15], (D, FF), D ** -0.5, 0.1875, ((1, 4),))
    down_weight = scatter_about(splits[16], (FF, D), FF ** -0.5, 0.109375, ((0, 4),))
    forget = jnp.clip(jax.random.uniform(splits[17], (HEADS,), jnp.float32, 0.5, 0.99), 0.5, 0.99)
    write_rate = jnp.clip(jax.random.uniform(splits[18], (HEADS,), jnp.float32, 0.1, 0.9), 0.1, 0.9)
    return {"tokens": tokens, "lengths": lengths, "prompt_group": prompt_group, "span_close": span_close, "out_slot": out_slot, "move_dest": move_dest, "page_table": page_table, "cache_pool": cache_pool, "prefix_cache": prefix_cache, "memory": memory, "norm_attn": norm_attn, "norm_mlp": norm_mlp, "qkv_weight": qkv_weight, "out_weight": out_weight, "gate_weight": gate_weight, "up_weight": up_weight, "down_weight": down_weight, "forget": forget, "write_rate": write_rate}


highest = lax.Precision.HIGHEST

def rms_scale(values, gain_vec):
    return values * lax.rsqrt(lax.optimization_barrier(jnp.mean(values * values, axis=-1, keepdims=True)) + 1e-05) * gain_vec

def unit_rows(values):
    return values * lax.rsqrt(lax.optimization_barrier(jnp.sum(values * values, axis=-1, keepdims=True)) + 1e-06)

def reference(tokens, lengths, prompt_group, span_close, out_slot, move_dest, page_table, cache_pool, prefix_cache, memory, norm_attn, norm_mlp, qkv_weight, out_weight, gate_weight, up_weight, down_weight, forget, write_rate):
    residual_in = tokens.astype(jnp.float32)
    normed = rms_scale(residual_in, norm_attn).astype(jnp.bfloat16)
    qkv_full = jnp.dot(normed, qkv_weight, preferred_element_type=jnp.float32).astype(jnp.bfloat16)
    queries = qkv_full[:, :D].reshape(REQUESTS, HEADS, HEAD).astype(jnp.float32)
    keys_new = qkv_full[:, D:2 * D].reshape(REQUESTS, HEADS, HEAD).astype(jnp.float32)
    values_new = qkv_full[:, 2 * D:].reshape(REQUESTS, HEADS, HEAD).astype(jnp.float32)
    score_scale = HEAD ** (-0.5)
    positions = ((2 * jnp.arange(HP)[None, :, None] + jnp.arange(2)[:, None, None]) * PAGE + jnp.arange(PAGE)[None, None, :]).reshape(-1)
    sect_half = jnp.arange(2 * HEADS) // HEADS

    def one_replica(inputs):
        pool_rows, table_rows, query_rows, key_rows, value_rows, length_rows, group_ids = inputs
        page_data = pool_rows[table_rows[:, sect_half, :], jnp.arange(2 * HEADS)[None, :, None]]
        page_data = page_data.reshape(REQ_DEV, 2, HEADS, HP * PAGE, 2 * HEAD).transpose(0, 2, 1, 3, 4)
        page_data = page_data.reshape(REQ_DEV, HEADS, 2 * HP * PAGE, 2 * HEAD).astype(jnp.float32)
        prefix = prefix_cache[group_ids].reshape(REQ_DEV, 2, HEADS, PREFIX // 2, 2 * HEAD).transpose(0, 2, 1, 3, 4)
        prefix = prefix.reshape(REQ_DEV, HEADS, PREFIX, 2 * HEAD).astype(jnp.float32)
        key_data = jnp.concatenate([prefix, page_data], axis=2)
        live_keys = jnp.concatenate([jnp.ones((REQ_DEV, PREFIX), bool), positions[None, :] < length_rows[:, None]], axis=1)[:, None, :]
        scores = jnp.einsum('rhd,rhnd->rhn', query_rows, key_data[..., :HEAD], precision=highest) * score_scale
        scores = jnp.where(live_keys, scores, -jnp.inf)
        own_score = lax.optimization_barrier(jnp.sum(query_rows * key_rows, axis=-1)) * score_scale
        top_score = jnp.maximum(lax.optimization_barrier(jnp.max(scores, axis=-1)), own_score)
        weights = jnp.exp(scores - top_score[..., None])
        own_weight = jnp.exp(own_score - top_score)
        denom_sum = lax.optimization_barrier(jnp.sum(weights, axis=-1)) + own_weight
        accumulated = jnp.einsum('rhn,rhnd->rhd', weights, key_data[..., HEAD:], precision=highest) + own_weight[..., None] * value_rows
        return accumulated / denom_sum[..., None]
    attended = lax.map(one_replica, (cache_pool.reshape(N_REP, POOL, 2 * HEADS, PAGE, 2 * HEAD), page_table.reshape(N_REP, REQ_DEV, 2, HP), queries.reshape(N_REP, REQ_DEV, HEADS, HEAD), keys_new.reshape(N_REP, REQ_DEV, HEADS, HEAD), values_new.reshape(N_REP, REQ_DEV, HEADS, HEAD), lengths.reshape(N_REP, REQ_DEV), prompt_group.reshape(N_REP, REQ_DEV))).reshape(REQUESTS, HEADS, HEAD)
    query_unit = unit_rows(queries)
    key_unit = unit_rows(keys_new)
    mem_full = memory.reshape(REQUESTS, 2, HEADS, HEAD // 2, HEAD).transpose(0, 2, 1, 3, 4).reshape(REQUESTS, HEADS, HEAD, HEAD)
    recalled = jnp.einsum('rhij,rhj->rhi', mem_full, query_unit, precision=highest)
    mixed_sum = (attended + recalled).reshape(REQUESTS, HEADS, 2, HEAD // 2).transpose(0, 2, 1, 3)
    mixed_out = mixed_sum.reshape(REQUESTS, D).astype(jnp.bfloat16)
    hidden_in = residual_in + jnp.dot(mixed_out, out_weight, preferred_element_type=jnp.float32)
    normed_mlp = rms_scale(hidden_in, norm_mlp).astype(jnp.bfloat16)
    gate_out = jnp.dot(normed_mlp, gate_weight, preferred_element_type=jnp.float32)
    up_out = jnp.dot(normed_mlp, up_weight, preferred_element_type=jnp.float32)
    activated = (jax.nn.silu(gate_out) * up_out).astype(jnp.bfloat16)
    rows_done = (hidden_in + jnp.dot(activated, down_weight, preferred_element_type=jnp.float32)).astype(jnp.bfloat16)
    predicted = jnp.einsum('rhij,rhj->rhi', mem_full, key_unit, precision=highest)
    misfit = values_new - predicted
    updated = forget[None, :, None, None] * mem_full + write_rate[None, :, None, None] * misfit[..., None] * key_unit[:, :, None, :]
    mem_after = jnp.where(span_close[:, None, None, None] == 1, updated, mem_full)
    mem_after = mem_after.reshape(REQUESTS, HEADS, 2, HEAD // 2, HEAD).transpose(0, 2, 1, 3, 4).reshape(memory.shape)
    src_rows = (jnp.arange(N_REP)[:, None] * REQ_DEV + out_slot).astype(jnp.int32)
    dst_rows = (move_dest * REQ_DEV + out_slot[move_dest, jnp.arange(MOVES)[None, :]]).astype(jnp.int32)
    new_from = jnp.arange(REQUESTS).astype(jnp.int32).at[dst_rows.reshape(-1)].set(src_rows.reshape(-1))
    src_pages = (jnp.arange(N_REP)[:, None, None, None] * POOL + page_table[src_rows][:, :, sect_half, :]).astype(jnp.int32)
    dst_pages = (move_dest[:, :, None, None] * POOL + page_table[dst_rows][:, :, sect_half, :]).astype(jnp.int32)
    sect_ids = jnp.arange(2 * HEADS).astype(jnp.int32)[None, None, :, None]
    new_pool = cache_pool.at[dst_pages, sect_ids].set(cache_pool[src_pages, sect_ids])
    return (rows_done[new_from], mem_after[new_from], new_pool)
```

```python
import functools
import math

import jax
import jax.numpy as jnp
from jax import lax
from jax.experimental import pallas as pl
from jax.experimental.pallas import tpu as pltpu
from jax.sharding import PartitionSpec as P

MESH = pl.DeviceIdType.MESH
f32, bf16, i32 = jnp.float32, jnp.bfloat16, jnp.int32
LOW = -1e30


def split2(x):
    hi = x.astype(bf16)
    lo = (x - hi.astype(f32)).astype(bf16)
    return hi, lo


def dot_t(a, b):
    return lax.dot_general(a, b, (((1,), (1,)), ((), ())), preferred_element_type=f32)


def rms_scale(values, gain_vec):
    return values * lax.rsqrt(jnp.mean(values * values, axis=-1, keepdims=True) + 1e-05) * gain_vec


def unit_rows(values):
    return values * lax.rsqrt(jnp.sum(values * values, axis=-1, keepdims=True) + 1e-06)


def column(ref_values, count):
    rows = lax.broadcasted_iota(i32, (count, 1), 0)
    out = jnp.zeros((count, 1), i32)
    for r in range(count):
        out = jnp.where(rows == r, ref_values(r), out)
    return out


def step_kernel(
    n_rep, n_tp,
    lengths, group, span, out_slot, move_dest, table, forget, rate,
    norm_attn, norm_mlp, tokens_hbm, qkvw_hbm, pool_hbm, prefix_hbm, mem_hbm,
    outw_hbm, gatew_hbm, upw_hbm, downw_hbm,
    rows_out, mem_after, mem_in, pages_in,
    tokens, qkvw, pool, prefix, mem, outw, gatew, upw, downw, mem_new,
    qbuf, dtab, part_send, part_recv, ar_one, ar_two, row_buf, held_page, held_mem,
    pick_page, pick_mem,
    load_sem, out_sem, q_send, q_recv, d_send, d_recv, part_sem, one_send, one_recv,
    two_send, two_recv, row_send, row_recv, page_send, page_recv, mem_send, mem_recv,
):
    n_req, model_dim = tokens.shape
    n_pool, n_sect, page_len, width = pool.shape
    head_dim = width // 2
    n_group, _, pre_len, _ = prefix.shape
    half_dim = mem.shape[2]
    n_head = model_dim // head_dim
    n_move = out_slot.shape[1]
    n_block, _, block = qbuf.shape
    own_blocks = n_block // n_tp
    per_head = head_dim // block
    routed = n_rep == 8
    scale = head_dim ** (-0.5)
    rep = lax.axis_index("rep")
    tp = lax.axis_index("tp")
    half = (tp * n_sect) // n_head

    def rep_flip(bits):
        return rep + bits * (1 - 2 * (lax.rem(lax.div(rep, bits), 2)))

    loads = []
    for i, (src, dst) in enumerate([
        (tokens_hbm, tokens), (qkvw_hbm, qkvw), (pool_hbm, pool), (prefix_hbm, prefix),
        (mem_hbm, mem), (outw_hbm, outw), (gatew_hbm, gatew), (upw_hbm, upw), (downw_hbm, downw),
    ]):
        copy = pltpu.make_async_copy(src, dst, load_sem.at[i])
        copy.start()
        loads.append(copy)

    barrier = pltpu.get_barrier_semaphore()
    for o in range(1, n_tp):
        pl.semaphore_signal(
            barrier, inc=1, device_id=(rep, lax.rem(tp + o, n_tp)), device_id_type=MESH
        )
    for o in range(1, n_rep):
        pl.semaphore_signal(
            barrier, inc=1, device_id=(lax.rem(rep + o, n_rep), tp), device_id_type=MESH
        )

    def tp_gather(buf_own, send, recv):
        copies = []
        for o in range(1, n_tp):
            copy = pltpu.make_async_remote_copy(
                src_ref=buf_own, dst_ref=buf_own, send_sem=send.at[o - 1], recv_sem=recv.at[o - 1],
                device_id=(rep, lax.rem(tp + o, n_tp)), device_id_type=MESH,
            )
            copy.start()
            copies.append(copy)
        return copies

    def rep_gather(buf_own, send, recv):
        copies = []
        for o in range(1, n_rep):
            copy = pltpu.make_async_remote_copy(
                src_ref=buf_own, dst_ref=buf_own, send_sem=send.at[o - 1], recv_sem=recv.at[o - 1],
                device_id=(lax.rem(rep + o, n_rep), tp), device_id_type=MESH,
            )
            copy.start()
            copies.append(copy)
        return copies

    def wait_all(copies):
        for copy in copies:
            copy.wait()

    loads[0].wait()
    residual = tokens[...].astype(f32)
    normed = rms_scale(residual, norm_attn[...]).astype(bf16)
    lane = lax.broadcasted_iota(i32, (8, 128), 1)
    tags = jnp.zeros((8, 128), i32)
    for m in range(n_move):
        tags = jnp.where(lane == m, move_dest[0, m], tags)
    dtab[rep] = tags
    loads[1].wait()
    qkv = jnp.dot(normed, qkvw[...], preferred_element_type=f32).astype(bf16)
    for b in range(own_blocks):
        qbuf[tp * own_blocks + b] = qkv[:, b * block:(b + 1) * block]

    pl.semaphore_wait(barrier, n_tp + n_rep - 2)
    q_copies = tp_gather(qbuf.at[pl.ds(tp * own_blocks, own_blocks)], q_send, q_recv)
    d_copies = rep_gather(dtab.at[rep], d_send, d_recv)

    def push(src, dst, send, recv, peer):
        copy = pltpu.make_async_remote_copy(
            src_ref=src, dst_ref=dst, send_sem=send, recv_sem=recv,
            device_id=(peer, tp), device_id_type=MESH,
        )
        copy.start()
        return copy

    first_bits, last_bits = (2, 4), (4, 2)

    def route_begin(held, send, recv):
        if not routed:
            return rep_gather(held.at[rep], send, recv)
        copies = []
        for k in range(2):
            copies.append(push(held.at[k, 0], held.at[k, 2], send.at[k, 0], recv.at[k, 0],
                               rep_flip(first_bits[k])))
        for k in range(2):
            copies.append(push(held.at[k, 0], held.at[k, 1], send.at[k, 1], recv.at[k, 1],
                               rep_flip(1)))
        return copies

    def route_forward(copies, held, send, recv):
        if not routed:
            return
        for k in range(2):
            copies[k].wait_recv()
            copies.append(push(held.at[k, 2], held.at[k, 3], send.at[k, 2], recv.at[k, 2],
                               rep_flip(1)))

    def dest_of(r, m):
        return dtab[r][0:1, m:m + 1]

    def slot_rep(k, j):
        there = rep if j < 2 else rep_flip(first_bits[k])
        if j % 2:
            there = there + 1 - 2 * lax.rem(there, 2)
        return there

    def choose(held, k, m, s, wanted):
        out = held[k, 0, m, s].astype(f32)
        for j in range(1, 4):
            out = jnp.where(dest_of(slot_rep(k, j), m) == wanted, held[k, j, m, s].astype(f32), out)
        return out

    def route_last(copies, held, pick, send, recv):
        if not routed:
            return
        for copy in copies[2:6]:
            copy.wait_recv()
        for k in range(2):
            peer = rep_flip(last_bits[k])
            for m in range(n_move):
                for s in range(n_sect):
                    pick[k, m, s] = choose(held, k, m, s, peer).astype(bf16)
            copies.append(push(pick.at[k], held.at[k, 4], send.at[k, 3], recv.at[k, 3], peer))

    def route_end(copies, held, out_ref):
        if not routed:
            wait_all(copies)
            for m in range(n_move):
                for s in range(n_sect):
                    def body(r, acc):
                        return jnp.where(dest_of(r, m) == rep, held[r, m, s].astype(f32), acc)
                    out_ref[m, s] = lax.fori_loop(
                        0, n_rep, body, jnp.zeros(out_ref.shape[2:], f32)
                    ).astype(out_ref.dtype)
            return
        for copy in copies[6:8]:
            copy.wait_recv()
        for copy in copies:
            copy.wait_send()
        rows = held.shape[4]
        for k in range(2):
            for m in range(n_move):
                for s in range(n_sect):
                    out = held[k, 4, m, s].astype(f32)
                    for j in range(4):
                        out = jnp.where(dest_of(slot_rep(k, j), m) == rep,
                                        held[k, j, m, s].astype(f32), out)
                    out_ref[m, s, pl.ds(k * rows, rows)] = out.astype(out_ref.dtype)

    loads[2].wait()
    for m in range(n_move):
        page = table[out_slot[0, m], half]
        for s in range(n_sect):
            leaving = pool[page, s]
            if routed:
                cut = page_len // 2
                held_page[0, 0, m, s] = leaving[:cut]
                held_page[1, 0, m, s] = leaving[cut:]
            else:
                held_page[rep, m, s] = leaving
    page_copies = route_begin(held_page, page_send, page_recv)

    page_col = column(lambda r: table[r, half], n_req)
    length_col = column(lambda r: lengths[r], n_req)
    group_col = column(lambda r: group[r], n_req)
    span_col = column(lambda r: span[r], n_req)
    keys_at = lax.broadcasted_iota(i32, (n_req, n_pool * page_len), 1)
    live_pool = (keys_at // page_len == page_col) & (
        keys_at % page_len + half * page_len < length_col
    )
    pre_at = lax.broadcasted_iota(i32, (n_req, n_group * pre_len), 1)
    live_pre = pre_at // pre_len == group_col
    loads[3].wait()
    wait_all(q_copies)

    def head_rows(base, s):
        head = lax.rem(tp * n_sect + s, n_head)
        parts = [qbuf[base * n_head * per_head + head * per_head + j] for j in range(per_head)]
        return parts[0] if per_head == 1 else jnp.concatenate(parts, axis=1)

    queries = [head_rows(0, s) for s in range(n_sect)]
    new_keys = [head_rows(1, s).astype(f32) for s in range(n_sect)]
    new_values = [head_rows(2, s).astype(f32) for s in range(n_sect)]
    wide = lax.broadcasted_iota(i32, (n_req, 128), 1)
    stats = jnp.zeros((n_req, 128), f32)
    tops, denoms, accs = [], [], []
    for s in range(n_sect):
        q = queries[s]
        k_pool = pool[:, s, :, :head_dim].reshape(n_pool * page_len, head_dim)
        v_pool = pool[:, s, :, head_dim:].reshape(n_pool * page_len, head_dim)
        k_pre = prefix[:, s, :, :head_dim].reshape(n_group * pre_len, head_dim)
        v_pre = prefix[:, s, :, head_dim:].reshape(n_group * pre_len, head_dim)
        s_pool = jnp.where(live_pool, dot_t(q, k_pool) * scale, LOW)
        s_pre = jnp.where(live_pre, dot_t(q, k_pre) * scale, LOW)
        own = jnp.sum(q.astype(f32) * new_keys[s], axis=-1, keepdims=True) * scale
        own = jnp.where(half == 0, own, LOW)
        top = jnp.maximum(jnp.max(s_pool, axis=-1, keepdims=True),
                          jnp.max(s_pre, axis=-1, keepdims=True))
        top = jnp.maximum(top, own)
        w_pool = jnp.exp(s_pool - top)
        w_pre = jnp.exp(s_pre - top)
        w_own = jnp.exp(own - top)
        denom = (jnp.sum(w_pool, axis=-1, keepdims=True) + jnp.sum(w_pre, axis=-1, keepdims=True)
                 + w_own)
        both = jnp.dot(jnp.concatenate(split2(w_pool), axis=0), v_pool, preferred_element_type=f32)
        both = both + jnp.dot(
            jnp.concatenate(split2(w_pre), axis=0), v_pre, preferred_element_type=f32
        )
        acc = both[:n_req] + both[n_req:] + w_own * new_values[s]
        part_send[s] = acc
        stats = jnp.where(wide == s, top, stats)
        stats = jnp.where(wide == 64 + s, denom, stats)
        tops.append(top)
        denoms.append(denom)
        accs.append(acc)
    part_send[n_sect] = stats
    partner = lax.rem(tp + n_tp // 2, n_tp)
    part_copy = pltpu.make_async_remote_copy(
        src_ref=part_send, dst_ref=part_recv, send_sem=part_sem.at[0], recv_sem=part_sem.at[1],
        device_id=(rep, partner), device_id_type=MESH,
    )
    part_copy.start()

    loads[4].wait()
    mem_at = lax.broadcasted_iota(i32, (n_req, n_req * half_dim), 1)
    mem_row = lax.broadcasted_iota(i32, (n_req, n_req * half_dim), 0)
    mine = mem_at // half_dim == mem_row
    writes = mine & (span_col == 1)
    recalls = []

    def own_half(x):
        return jnp.where(half == 0, x[:, :half_dim], x[:, half_dim:])

    for s in range(n_sect):
        head = lax.rem(tp * n_sect + s, n_head)
        q_hi, q_lo = split2(unit_rows(queries[s].astype(f32)))
        k_hi, k_lo = split2(unit_rows(new_keys[s]))
        m_hi, m_lo = split2(mem[:, s].reshape(n_req * half_dim, head_dim))
        by_hi = dot_t(jnp.concatenate([q_hi, k_hi, q_lo, k_lo], axis=0), m_hi)
        by_lo = dot_t(jnp.concatenate([q_hi, k_hi], axis=0), m_lo)
        seen = by_hi[:2 * n_req] + by_hi[2 * n_req:] + by_lo
        recalled = jnp.where(mine, seen[:n_req], 0.0)
        fold = recalled[:, :128]
        for c in range(1, n_req * half_dim // 128):
            fold = fold + recalled[:, c * 128:(c + 1) * 128]
        recalls.append(fold[:, :half_dim] + fold[:, half_dim:])
        value = own_half(new_values[s])
        value = jnp.concatenate([value] * (n_req), axis=1)
        miss = jnp.where(writes, rate[head] * (value - seen[n_req:]), 0.0)
        miss_hi = miss.astype(bf16).astype(f32)
        stack = jnp.concatenate([miss_hi, miss - miss_hi, miss_hi], axis=0)
        grow = jnp.dot(
            jnp.transpose(stack).astype(bf16), jnp.concatenate([k_hi, k_hi, k_lo], axis=0),
            preferred_element_type=f32,
        )
        keep = forget[head]
        for r in range(n_req):
            kept = jnp.where(span[r] == 1, keep, 1.0)
            mem_new[r, s] = kept * mem[r, s] + grow[r * half_dim:(r + 1) * half_dim]
    mem_copy = pltpu.make_async_copy(mem_new, mem_after, out_sem)
    mem_copy.start()
    for m in range(n_move):
        for s in range(n_sect):
            leaving = mem_new[out_slot[0, m], s].astype(bf16)
            if routed:
                cut = half_dim // 2
                held_mem[0, 0, m, s] = leaving[:cut]
                held_mem[1, 0, m, s] = leaving[cut:]
            else:
                held_mem[rep, m, s] = leaving
    mem_copies = route_begin(held_mem, mem_send, mem_recv)

    part_copy.wait()
    theirs = part_recv[n_sect]
    mixed = []
    for s in range(n_sect):
        top_b = jnp.sum(jnp.where(wide == s, theirs, 0.0), axis=-1, keepdims=True)
        den_b = jnp.sum(jnp.where(wide == 64 + s, theirs, 0.0), axis=-1, keepdims=True)
        top = jnp.maximum(tops[s], top_b)
        w_a, w_b = jnp.exp(tops[s] - top), jnp.exp(top_b - top)
        total = accs[s] * w_a + part_recv[s] * w_b
        attended = total / (denoms[s] * w_a + den_b * w_b)
        mixed.append(own_half(attended) + recalls[s])
    mixed = mixed[0] if n_sect == 1 else jnp.concatenate(mixed, axis=1)
    loads[5].wait()
    ar_one[tp] = jnp.dot(mixed.astype(bf16), outw[...], preferred_element_type=f32).astype(bf16)
    one_copies = tp_gather(ar_one.at[tp], one_send, one_recv)
    wait_all(d_copies)
    route_forward(page_copies, held_page, page_send, page_recv)
    wait_all(one_copies)
    hidden = residual
    for t in range(n_tp):
        hidden = hidden + ar_one[t].astype(f32)
    normed = rms_scale(hidden, norm_mlp[...]).astype(bf16)
    loads[6].wait()
    gate = jnp.dot(normed, gatew[...], preferred_element_type=f32)
    loads[7].wait()
    up = jnp.dot(normed, upw[...], preferred_element_type=f32)
    activated = (gate * jax.nn.sigmoid(gate) * up).astype(bf16)
    loads[8].wait()
    ar_two[tp] = jnp.dot(activated, downw[...], preferred_element_type=f32).astype(bf16)
    two_copies = tp_gather(ar_two.at[tp], two_send, two_recv)
    route_last(page_copies, held_page, pick_page, page_send, page_recv)
    route_forward(mem_copies, held_mem, mem_send, mem_recv)
    wait_all(two_copies)
    total = ar_two[0].astype(f32)
    for t in range(1, n_tp):
        total = total + ar_two[t].astype(f32)
    rows = (hidden + total).astype(bf16)

    n_piece = model_dim // 128
    row_len = row_buf.shape[1]
    to_buf = lax.broadcasted_iota(i32, (row_len, n_req), 0)
    from_slot = lax.broadcasted_iota(i32, (row_len, n_req), 1)
    packed = jnp.zeros((row_len, 128), f32)
    for c in range(n_piece):
        hot = jnp.zeros((row_len, n_req), f32)
        for m in range(n_move):
            hot = jnp.where((to_buf == c * n_move + m) & (from_slot == out_slot[0, m]), 1.0, hot)
        packed = packed + jnp.dot(
            hot.astype(bf16), rows[:, c * 128:(c + 1) * 128], preferred_element_type=f32
        )
    row_buf[rep] = packed.astype(bf16)
    row_copies = rep_gather(row_buf.at[rep], row_send, row_recv)
    route_last(mem_copies, held_mem, pick_mem, mem_send, mem_recv)
    route_end(page_copies, held_page, pages_in)
    wait_all(row_copies)
    arrived = row_buf[...].reshape(n_rep * row_len, 128)
    slot_at = lax.broadcasted_iota(i32, (n_req, row_len), 0)
    buf_at = lax.broadcasted_iota(i32, (n_req, row_len), 1)
    slot_col = lax.broadcasted_iota(i32, (n_req, 1), 0)
    staying = jnp.ones((n_req, 1), jnp.bool_)
    for m in range(n_move):
        staying = staying & (slot_col != out_slot[0, m])
    chosen = jnp.zeros((row_len, 128), f32)
    buf_move = lax.broadcasted_iota(i32, (row_len, 128), 0) % n_move
    for r in range(n_rep):
        hit = jnp.zeros((row_len, 128), i32)
        for m in range(n_move):
            hit = jnp.where((buf_move == m) & (dest_of(r, m) == rep), 1, hit)
        chosen = jnp.where(hit == 1, row_buf[r].astype(f32), chosen)
    chosen = chosen.astype(bf16)
    for c in range(n_piece):
        hot = jnp.zeros((n_req, row_len), f32)
        for m in range(n_move):
            hot = jnp.where((buf_at == c * n_move + m) & (slot_at == out_slot[0, m]), 1.0, hot)
        came = jnp.dot(hot.astype(bf16), chosen, preferred_element_type=f32)
        kept = rows[:, c * 128:(c + 1) * 128].astype(f32)
        rows_out[:, c * 128:(c + 1) * 128] = jnp.where(staying, kept, came).astype(bf16)
    route_end(mem_copies, held_mem, mem_in)
    mem_copy.wait()


def place_kernel(
    table, out_slot, rows, pool, pages_in, mem, mem_in, rows_out, pool_out, mem_out,
    page_sem, mem_sem,
):
    n_pool, n_sect = pool.shape[0], pool.shape[1]
    n_req = mem.shape[0]
    n_head = rows.shape[1] // mem.shape[3]
    n_move = out_slot.shape[1]
    half = (lax.axis_index("tp") * n_sect) // n_head
    slots = [out_slot[0, m] for m in range(n_move)]
    pages = [table[slot, half] for slot in slots]

    def put(index, moved, kept, arrived, out, sem):
        stays = index >= 0
        for m in range(n_move):
            stays = stays & (index != moved[m])

            @pl.when(index == moved[m])
            def _(m=m):
                pltpu.make_async_copy(arrived.at[m], out.at[index], sem).start()

        @pl.when(stays)
        def _():
            pltpu.make_async_copy(kept.at[index], out.at[index], sem).start()

    for p in range(n_pool):
        put(jnp.int32(p), pages, pool, pages_in, pool_out, page_sem.at[p])
    for r in range(n_req):
        put(jnp.int32(r), slots, mem, mem_in, mem_out, mem_sem.at[r])
    rows_out[...] = rows[...]
    for p in range(n_pool):
        pltpu.make_async_copy(pool.at[p], pool_out.at[p], page_sem.at[p]).wait()
    for r in range(n_req):
        pltpu.make_async_copy(mem.at[r], mem_out.at[r], mem_sem.at[r]).wait()


def body(
    n_rep, n_tp, tokens, lengths, prompt_group, span_close, out_slot, move_dest, page_table,
    cache_pool, prefix_cache, memory, norm_attn, norm_mlp, qkv_weight, out_weight, gate_weight,
    up_weight, down_weight, forget, write_rate,
):
    n_req, model_dim = tokens.shape
    n_pool, n_sect, page_len, width = cache_pool.shape
    half_dim, head_dim = memory.shape[2:]
    n_move = out_slot.shape[1]
    columns = qkv_weight.shape[1]
    block = math.gcd(columns, head_dim)
    row_len = n_move * model_dim // 128
    table = page_table[:, :, 0]
    smem = pl.BlockSpec(memory_space=pltpu.SMEM)
    vmem = pl.BlockSpec(memory_space=pltpu.VMEM)
    anym = pl.BlockSpec(memory_space=pl.ANY)
    if n_rep == 8:
        lead, moved_sems = (2, 5), (2, 4)
        page_piece = (n_move, n_sect, page_len // 2, width)
        mem_piece = (n_move, n_sect, half_dim // 2, head_dim)
        picks = (2,)
    else:
        lead, moved_sems = (n_rep,), (n_rep - 1,)
        page_piece = (n_move, n_sect, page_len, width)
        mem_piece = (n_move, n_sect, half_dim, head_dim)
        picks = ()
    page_pick = picks + page_piece if picks else (8, 128)
    mem_pick = picks + mem_piece if picks else (8, 128)
    V, dma = pltpu.VMEM, pltpu.SemaphoreType.DMA
    whole = [tokens, qkv_weight, cache_pool, prefix_cache, memory, out_weight, gate_weight,
             up_weight, down_weight]
    rows, mem_after, mem_in, pages_in = pl.pallas_call(
        functools.partial(step_kernel, n_rep, n_tp),
        out_shape=(
            jax.ShapeDtypeStruct((n_req, model_dim), bf16),
            jax.ShapeDtypeStruct(memory.shape, f32),
            jax.ShapeDtypeStruct((n_move,) + memory.shape[1:], f32),
            jax.ShapeDtypeStruct((n_move,) + cache_pool.shape[1:], bf16),
        ),
        in_specs=[smem] * 8 + [vmem] * 2 + [anym] * 9,
        out_specs=(vmem, anym, vmem, vmem),
        scratch_shapes=[V(a.shape, a.dtype) for a in whole] + [
            V(memory.shape, f32),
            V((n_tp * columns // block, n_req, block), bf16),
            V((n_rep, 8, 128), i32),
            V((n_sect + 1, n_req, 128), f32),
            V((n_sect + 1, n_req, 128), f32),
            V((n_tp, n_req, model_dim), bf16),
            V((n_tp, n_req, model_dim), bf16),
            V((n_rep, row_len, 128), bf16),
            V(lead + page_piece, bf16),
            V(lead + mem_piece, bf16),
            V(page_pick, bf16),
            V(mem_pick, bf16),
            dma((9,)), dma,
            dma((n_tp - 1,)), dma((n_tp - 1,)),
            dma((n_rep - 1,)), dma((n_rep - 1,)),
            dma((2,)),
            dma((n_tp - 1,)), dma((n_tp - 1,)),
            dma((n_tp - 1,)), dma((n_tp - 1,)),
            dma((n_rep - 1,)), dma((n_rep - 1,)),
            dma(moved_sems), dma(moved_sems),
            dma(moved_sems), dma(moved_sems),
        ],
        compiler_params=pltpu.CompilerParams(
            collective_id=0, has_side_effects=True, vmem_limit_bytes=48 * 1024 * 1024
        ),
        name="step",
    )(lengths, prompt_group, span_close, out_slot, move_dest, table, forget, write_rate,
      norm_attn.reshape(1, model_dim), norm_mlp.reshape(1, model_dim), *whole)
    return pl.pallas_call(
        place_kernel,
        out_shape=(
            jax.ShapeDtypeStruct(rows.shape, bf16),
            jax.ShapeDtypeStruct(cache_pool.shape, bf16),
            jax.ShapeDtypeStruct(memory.shape, f32),
        ),
        in_specs=[smem] * 2 + [vmem] + [anym] * 4,
        out_specs=(vmem, anym, anym),
        scratch_shapes=[dma((n_pool,)), dma((n_req,))],
        name="place",
    )(table, out_slot, rows, cache_pool, pages_in, mem_after, mem_in)


def solution(mesh):
    row = P("rep", None)
    grid = P("rep", "tp", None, None)
    placed = (
        row, P("rep"), P("rep"), P("rep"), row, row, P("rep", None, None), grid,
        P(None, "tp", None, None), grid, P(), P(), P(None, "tp"), P("tp", None), P(None, "tp"),
        P(None, "tp"), P("tp", None), P(), P(),
    )

    def run(*args):
        rows, pool, mem = body(mesh.shape["rep"], mesh.shape["tp"], *args)
        return rows, mem, pool

    return jax.shard_map(
        run, mesh=mesh, in_specs=placed, out_specs=(row, grid, grid), check_vma=False
    )
```

```python
import functools
import math

import jax
import jax.numpy as jnp
from jax import lax
from jax.experimental import pallas as pl
from jax.experimental.pallas import tpu as pltpu
from jax.sharding import PartitionSpec as P

MESH = pl.DeviceIdType.MESH
f32, bf16, i32 = jnp.float32, jnp.bfloat16, jnp.int32
LOW = -1e30
VMEM_BYTES = 64 * 1024 * 1024


def split2(x):
    hi = x.astype(bf16)
    lo = (x - hi.astype(f32)).astype(bf16)
    return hi, lo


def dot_t(a, b):
    return lax.dot_general(a, b, (((1,), (1,)), ((), ())), preferred_element_type=f32)


def rms_scale(values, gain_vec):
    return values * lax.rsqrt(jnp.mean(values * values, axis=-1, keepdims=True) + 1e-05) * gain_vec


def unit_rows(values):
    return values * lax.rsqrt(jnp.sum(values * values, axis=-1, keepdims=True) + 1e-06)


def column(ref_values, count):
    rows = lax.broadcasted_iota(i32, (count, 1), 0)
    out = jnp.zeros((count, 1), i32)
    for r in range(count):
        out = jnp.where(rows == r, ref_values(r), out)
    return out


def step_kernel(
    n_rep, n_tp,
    lengths_hbm, group_hbm, span_hbm, out_slot_hbm, move_dest_hbm, table_hbm, forget_hbm,
    rate_hbm, norm_attn_hbm, norm_mlp_hbm, tokens_hbm, qkvw_hbm, pool_hbm, prefix_hbm, mem_hbm,
    outw_hbm, gatew_hbm, upw_hbm, downw_hbm,
    rows_out, mem_after, mem_in, pages_in,
    lengths, group, span, out_slot, move_dest, table, forget, rate,
    norm_attn, norm_mlp, tokens, qkvw, pool, prefix, mem, outw, gatew, upw, downw, mem_new,
    qbuf, dtab, part_send, part_recv, ar_one, ar_two, row_buf, held_page, held_mem,
    pick_page, pick_mem,
    small_sem, load_sem, out_sem, q_send, q_recv, d_send, d_recv, part_sem, one_send, one_recv,
    two_send, two_recv, row_send, row_recv, page_send, page_recv, mem_send, mem_recv,
):
    n_req, model_dim = tokens.shape
    n_pool, n_sect, page_len, width = pool.shape
    head_dim = width // 2
    n_group, _, pre_len, _ = prefix.shape
    half_dim = mem.shape[2]
    n_head = model_dim // head_dim
    n_move = out_slot.shape[1]
    n_block, _, block = qbuf.shape
    own_blocks = n_block // n_tp
    per_head = head_dim // block
    routed = n_rep == 8
    scale = head_dim ** (-0.5)
    rep = lax.axis_index("rep")
    tp = lax.axis_index("tp")
    half = (tp * n_sect) // n_head

    def rep_flip(bits):
        return rep + bits * (1 - 2 * (lax.rem(lax.div(rep, bits), 2)))

    smalls = []
    for i, (src, dst) in enumerate([
        (norm_attn_hbm, norm_attn), (move_dest_hbm, move_dest), (out_slot_hbm, out_slot),
        (table_hbm, table), (lengths_hbm, lengths), (group_hbm, group), (span_hbm, span),
        (forget_hbm, forget), (rate_hbm, rate), (norm_mlp_hbm, norm_mlp),
    ]):
        copy = pltpu.make_async_copy(src, dst, small_sem.at[i])
        copy.start()
        smalls.append(copy)
    loads = []
    for i, (src, dst) in enumerate([
        (tokens_hbm, tokens), (qkvw_hbm, qkvw), (pool_hbm, pool), (prefix_hbm, prefix),
        (mem_hbm, mem), (outw_hbm, outw), (gatew_hbm, gatew), (upw_hbm, upw), (downw_hbm, downw),
    ]):
        copy = pltpu.make_async_copy(src, dst, load_sem.at[i])
        copy.start()
        loads.append(copy)

    barrier = pltpu.get_barrier_semaphore()
    for o in range(1, n_tp):
        pl.semaphore_signal(
            barrier, inc=1, device_id=(rep, lax.rem(tp + o, n_tp)), device_id_type=MESH
        )
    for o in range(1, n_rep):
        pl.semaphore_signal(
            barrier, inc=1, device_id=(lax.rem(rep + o, n_rep), tp), device_id_type=MESH
        )

    def tp_gather(buf_own, send, recv):
        copies = []
        for o in range(1, n_tp):
            copy = pltpu.make_async_remote_copy(
                src_ref=buf_own, dst_ref=buf_own, send_sem=send.at[o - 1], recv_sem=recv.at[o - 1],
                device_id=(rep, lax.rem(tp + o, n_tp)), device_id_type=MESH,
            )
            copy.start()
            copies.append(copy)
        return copies

    def rep_gather(buf_own, send, recv):
        copies = []
        for o in range(1, n_rep):
            copy = pltpu.make_async_remote_copy(
                src_ref=buf_own, dst_ref=buf_own, send_sem=send.at[o - 1], recv_sem=recv.at[o - 1],
                device_id=(lax.rem(rep + o, n_rep), tp), device_id_type=MESH,
            )
            copy.start()
            copies.append(copy)
        return copies

    def wait_all(copies):
        for copy in copies:
            copy.wait()

    wait_all(smalls)
    loads[0].wait()
    residual = tokens[...].astype(f32)
    normed = rms_scale(residual, norm_attn[...]).astype(bf16)
    lane = lax.broadcasted_iota(i32, (8, 128), 1)
    tags = jnp.zeros((8, 128), i32)
    for m in range(n_move):
        tags = jnp.where(lane == m, move_dest[0, m], tags)
    dtab[rep] = tags
    loads[1].wait()
    qkv = jnp.dot(normed, qkvw[...], preferred_element_type=f32).astype(bf16)
    for b in range(own_blocks):
        qbuf[tp * own_blocks + b] = qkv[:, b * block:(b + 1) * block]

    pl.semaphore_wait(barrier, n_tp + n_rep - 2)
    q_copies = tp_gather(qbuf.at[pl.ds(tp * own_blocks, own_blocks)], q_send, q_recv)
    d_copies = rep_gather(dtab.at[rep], d_send, d_recv)

    def push(src, dst, send, recv, peer):
        copy = pltpu.make_async_remote_copy(
            src_ref=src, dst_ref=dst, send_sem=send, recv_sem=recv,
            device_id=(peer, tp), device_id_type=MESH,
        )
        copy.start()
        return copy

    first_bits, last_bits = (2, 4), (4, 2)

    def route_begin(held, send, recv):
        if not routed:
            return rep_gather(held.at[rep], send, recv)
        copies = []
        for k in range(2):
            copies.append(push(held.at[k, 0], held.at[k, 2], send.at[k, 0], recv.at[k, 0],
                               rep_flip(first_bits[k])))
        for k in range(2):
            copies.append(push(held.at[k, 0], held.at[k, 1], send.at[k, 1], recv.at[k, 1],
                               rep_flip(1)))
        return copies

    def route_forward(copies, held, send, recv):
        if not routed:
            return
        for k in range(2):
            copies[k].wait_recv()
            copies.append(push(held.at[k, 2], held.at[k, 3], send.at[k, 2], recv.at[k, 2],
                               rep_flip(1)))

    def dest_of(r, m):
        return dtab[r][0:1, m:m + 1]

    def slot_rep(k, j):
        there = rep if j < 2 else rep_flip(first_bits[k])
        if j % 2:
            there = there + 1 - 2 * lax.rem(there, 2)
        return there

    def choose(held, k, m, s, wanted):
        out = held[k, 0, m, s].astype(f32)
        for j in range(1, 4):
            out = jnp.where(dest_of(slot_rep(k, j), m) == wanted, held[k, j, m, s].astype(f32), out)
        return out

    def route_last(copies, held, pick, send, recv):
        if not routed:
            return
        for copy in copies[2:6]:
            copy.wait_recv()
        for k in range(2):
            peer = rep_flip(last_bits[k])
            for m in range(n_move):
                for s in range(n_sect):
                    pick[k, m, s] = choose(held, k, m, s, peer).astype(bf16)
            copies.append(push(pick.at[k], held.at[k, 4], send.at[k, 3], recv.at[k, 3], peer))

    def route_end(copies, held, out_ref):
        if not routed:
            wait_all(copies)
            for m in range(n_move):
                for s in range(n_sect):
                    def body(r, acc):
                        return jnp.where(dest_of(r, m) == rep, held[r, m, s].astype(f32), acc)
                    out_ref[m, s] = lax.fori_loop(
                        0, n_rep, body, jnp.zeros(out_ref.shape[2:], f32)
                    ).astype(out_ref.dtype)
            return
        for copy in copies[6:8]:
            copy.wait_recv()
        for copy in copies:
            copy.wait_send()
        rows = held.shape[4]
        for k in range(2):
            for m in range(n_move):
                for s in range(n_sect):
                    out = held[k, 4, m, s].astype(f32)
                    for j in range(4):
                        out = jnp.where(dest_of(slot_rep(k, j), m) == rep,
                                        held[k, j, m, s].astype(f32), out)
                    out_ref[m, s, pl.ds(k * rows, rows)] = out.astype(out_ref.dtype)

    loads[2].wait()
    for m in range(n_move):
        page = table[half, out_slot[0, m]]
        for s in range(n_sect):
            leaving = pool[page, s]
            if routed:
                cut = page_len // 2
                held_page[0, 0, m, s] = leaving[:cut]
                held_page[1, 0, m, s] = leaving[cut:]
            else:
                held_page[rep, m, s] = leaving
    page_copies = route_begin(held_page, page_send, page_recv)

    page_col = column(lambda r: table[half, r], n_req)
    length_col = column(lambda r: lengths[r], n_req)
    group_col = column(lambda r: group[r], n_req)
    span_col = column(lambda r: span[r], n_req)
    keys_at = lax.broadcasted_iota(i32, (n_req, n_pool * page_len), 1)
    live_pool = (keys_at // page_len == page_col) & (
        keys_at % page_len + half * page_len < length_col
    )
    pre_at = lax.broadcasted_iota(i32, (n_req, n_group * pre_len), 1)
    live_pre = pre_at // pre_len == group_col
    loads[3].wait()
    wait_all(q_copies)

    def head_rows(base, s):
        head = lax.rem(tp * n_sect + s, n_head)
        parts = [qbuf[base * n_head * per_head + head * per_head + j] for j in range(per_head)]
        return parts[0] if per_head == 1 else jnp.concatenate(parts, axis=1)

    queries = [head_rows(0, s) for s in range(n_sect)]
    new_keys = [head_rows(1, s).astype(f32) for s in range(n_sect)]
    new_values = [head_rows(2, s).astype(f32) for s in range(n_sect)]
    wide = lax.broadcasted_iota(i32, (n_req, 128), 1)
    stats = jnp.zeros((n_req, 128), f32)
    tops, denoms, accs = [], [], []
    for s in range(n_sect):
        q = queries[s]
        k_pool = pool[:, s, :, :head_dim].reshape(n_pool * page_len, head_dim)
        v_pool = pool[:, s, :, head_dim:].reshape(n_pool * page_len, head_dim)
        k_pre = prefix[:, s, :, :head_dim].reshape(n_group * pre_len, head_dim)
        v_pre = prefix[:, s, :, head_dim:].reshape(n_group * pre_len, head_dim)
        s_pool = jnp.where(live_pool, dot_t(q, k_pool) * scale, LOW)
        s_pre = jnp.where(live_pre, dot_t(q, k_pre) * scale, LOW)
        own = jnp.sum(q.astype(f32) * new_keys[s], axis=-1, keepdims=True) * scale
        own = jnp.where(half == 0, own, LOW)
        top = jnp.maximum(jnp.max(s_pool, axis=-1, keepdims=True),
                          jnp.max(s_pre, axis=-1, keepdims=True))
        top = jnp.maximum(top, own)
        w_pool = jnp.exp(s_pool - top)
        w_pre = jnp.exp(s_pre - top)
        w_own = jnp.exp(own - top)
        denom = (jnp.sum(w_pool, axis=-1, keepdims=True) + jnp.sum(w_pre, axis=-1, keepdims=True)
                 + w_own)
        both = jnp.dot(jnp.concatenate(split2(w_pool), axis=0), v_pool, preferred_element_type=f32)
        both = both + jnp.dot(
            jnp.concatenate(split2(w_pre), axis=0), v_pre, preferred_element_type=f32
        )
        acc = both[:n_req] + both[n_req:] + w_own * new_values[s]
        part_send[s] = acc
        stats = jnp.where(wide == s, top, stats)
        stats = jnp.where(wide == 64 + s, denom, stats)
        tops.append(top)
        denoms.append(denom)
        accs.append(acc)
    part_send[n_sect] = stats
    partner = lax.rem(tp + n_tp // 2, n_tp)
    part_copy = pltpu.make_async_remote_copy(
        src_ref=part_send, dst_ref=part_recv, send_sem=part_sem.at[0], recv_sem=part_sem.at[1],
        device_id=(rep, partner), device_id_type=MESH,
    )
    part_copy.start()

    loads[4].wait()
    mem_at = lax.broadcasted_iota(i32, (n_req, n_req * half_dim), 1)
    mem_row = lax.broadcasted_iota(i32, (n_req, n_req * half_dim), 0)
    mine = mem_at // half_dim == mem_row
    writes = mine & (span_col == 1)
    recalls, predicts, units = [], [], []

    def own_half(x):
        return jnp.where(half == 0, x[:, :half_dim], x[:, half_dim:])

    for s in range(n_sect):
        q_hi, q_lo = split2(unit_rows(queries[s].astype(f32)))
        k_hi, k_lo = split2(unit_rows(new_keys[s]))
        m_hi, m_lo = split2(mem[:, s].reshape(n_req * half_dim, head_dim))
        by_hi = dot_t(jnp.concatenate([q_hi, k_hi, q_lo, k_lo], axis=0), m_hi)
        by_lo = dot_t(jnp.concatenate([q_hi, k_hi], axis=0), m_lo)
        seen = by_hi[:2 * n_req] + by_hi[2 * n_req:] + by_lo
        recalled = jnp.where(mine, seen[:n_req], 0.0)
        fold = recalled[:, :128]
        for c in range(1, n_req * half_dim // 128):
            fold = fold + recalled[:, c * 128:(c + 1) * 128]
        recalls.append(fold[:, :half_dim] + fold[:, half_dim:])
        predicts.append(seen[n_req:])
        units.append((k_hi, k_lo))
    wait_all(d_copies)
    route_forward(page_copies, held_page, page_send, page_recv)

    part_copy.wait()
    theirs = part_recv[n_sect]
    mixed = []
    for s in range(n_sect):
        top_b = jnp.sum(jnp.where(wide == s, theirs, 0.0), axis=-1, keepdims=True)
        den_b = jnp.sum(jnp.where(wide == 64 + s, theirs, 0.0), axis=-1, keepdims=True)
        top = jnp.maximum(tops[s], top_b)
        w_a, w_b = jnp.exp(tops[s] - top), jnp.exp(top_b - top)
        total = accs[s] * w_a + part_recv[s] * w_b
        attended = total / (denoms[s] * w_a + den_b * w_b)
        mixed.append(own_half(attended) + recalls[s])
    mixed = mixed[0] if n_sect == 1 else jnp.concatenate(mixed, axis=1)
    loads[5].wait()
    ar_one[tp] = jnp.dot(mixed.astype(bf16), outw[...], preferred_element_type=f32).astype(bf16)
    one_copies = tp_gather(ar_one.at[tp], one_send, one_recv)
    route_last(page_copies, held_page, pick_page, page_send, page_recv)

    for s in range(n_sect):
        head = lax.rem(tp * n_sect + s, n_head)
        k_hi, k_lo = units[s]
        value = jnp.concatenate([own_half(new_values[s])] * n_req, axis=1)
        miss = jnp.where(writes, rate[head] * (value - predicts[s]), 0.0)
        miss_hi = miss.astype(bf16).astype(f32)
        stack = jnp.concatenate([miss_hi, miss - miss_hi, miss_hi], axis=0)
        grow = jnp.dot(
            jnp.transpose(stack).astype(bf16), jnp.concatenate([k_hi, k_hi, k_lo], axis=0),
            preferred_element_type=f32,
        )
        keep = forget[head]
        for r in range(n_req):
            kept = jnp.where(span[r] == 1, keep, 1.0)
            mem_new[r, s] = kept * mem[r, s] + grow[r * half_dim:(r + 1) * half_dim]
    mem_copy = pltpu.make_async_copy(mem_new, mem_after, out_sem)
    mem_copy.start()
    for m in range(n_move):
        for s in range(n_sect):
            leaving = mem_new[out_slot[0, m], s].astype(bf16)
            if routed:
                cut = half_dim // 2
                held_mem[0, 0, m, s] = leaving[:cut]
                held_mem[1, 0, m, s] = leaving[cut:]
            else:
                held_mem[rep, m, s] = leaving
    mem_copies = route_begin(held_mem, mem_send, mem_recv)
    wait_all(one_copies)
    hidden = residual
    for t in range(n_tp):
        hidden = hidden + ar_one[t].astype(f32)
    normed = rms_scale(hidden, norm_mlp[...]).astype(bf16)
    loads[6].wait()
    gate = dot_t(normed, gatew[...])
    loads[7].wait()
    up = dot_t(normed, upw[...])
    activated = (gate * jax.nn.sigmoid(gate) * up).astype(bf16)
    loads[8].wait()
    ar_two[tp] = jnp.dot(activated, downw[...], preferred_element_type=f32).astype(bf16)
    two_copies = tp_gather(ar_two.at[tp], two_send, two_recv)
    route_forward(mem_copies, held_mem, mem_send, mem_recv)
    wait_all(two_copies)
    total = ar_two[0].astype(f32)
    for t in range(1, n_tp):
        total = total + ar_two[t].astype(f32)
    rows = (hidden + total).astype(bf16)

    n_piece = model_dim // 128
    row_len = row_buf.shape[1]
    to_buf = lax.broadcasted_iota(i32, (row_len, n_req), 0)
    from_slot = lax.broadcasted_iota(i32, (row_len, n_req), 1)
    packed = jnp.zeros((row_len, 128), f32)
    for c in range(n_piece):
        hot = jnp.zeros((row_len, n_req), f32)
        for m in range(n_move):
            hot = jnp.where((to_buf == c * n_move + m) & (from_slot == out_slot[0, m]), 1.0, hot)
        packed = packed + jnp.dot(
            hot.astype(bf16), rows[:, c * 128:(c + 1) * 128], preferred_element_type=f32
        )
    row_buf[rep] = packed.astype(bf16)
    row_copies = rep_gather(row_buf.at[rep], row_send, row_recv)
    route_last(mem_copies, held_mem, pick_mem, mem_send, mem_recv)
    route_end(page_copies, held_page, pages_in)
    wait_all(row_copies)
    arrived = row_buf[...].reshape(n_rep * row_len, 128)
    slot_at = lax.broadcasted_iota(i32, (n_req, row_len), 0)
    buf_at = lax.broadcasted_iota(i32, (n_req, row_len), 1)
    slot_col = lax.broadcasted_iota(i32, (n_req, 1), 0)
    staying = jnp.ones((n_req, 1), jnp.bool_)
    for m in range(n_move):
        staying = staying & (slot_col != out_slot[0, m])
    chosen = jnp.zeros((row_len, 128), f32)
    buf_move = lax.broadcasted_iota(i32, (row_len, 128), 0) % n_move
    for r in range(n_rep):
        hit = jnp.zeros((row_len, 128), i32)
        for m in range(n_move):
            hit = jnp.where((buf_move == m) & (dest_of(r, m) == rep), 1, hit)
        chosen = jnp.where(hit == 1, row_buf[r].astype(f32), chosen)
    chosen = chosen.astype(bf16)
    for c in range(n_piece):
        hot = jnp.zeros((n_req, row_len), f32)
        for m in range(n_move):
            hot = jnp.where((buf_at == c * n_move + m) & (slot_at == out_slot[0, m]), 1.0, hot)
        came = jnp.dot(hot.astype(bf16), chosen, preferred_element_type=f32)
        kept = rows[:, c * 128:(c + 1) * 128].astype(f32)
        rows_out[:, c * 128:(c + 1) * 128] = jnp.where(staying, kept, came).astype(bf16)
    route_end(mem_copies, held_mem, mem_in)
    mem_copy.wait()


def place_kernel(
    table_hbm, out_slot_hbm, rows_hbm, pool, pages_in, mem, mem_in, rows_out, pool_out, mem_out,
    table, out_slot, page_buf, mem_buf, small_sem, page_load, mem_load, page_sem, mem_sem,
):
    smalls = [
        pltpu.make_async_copy(table_hbm, table, small_sem.at[0]),
        pltpu.make_async_copy(out_slot_hbm, out_slot, small_sem.at[1]),
        pltpu.make_async_copy(rows_hbm, rows_out, small_sem.at[2]),
    ]
    for copy in smalls:
        copy.start()
    n_pool, n_sect = pool.shape[0], pool.shape[1]
    n_req = mem.shape[0]
    n_head = rows_hbm.shape[1] // mem.shape[3]
    n_move = out_slot.shape[1]
    half = (lax.axis_index("tp") * n_sect) // n_head
    for copy in smalls[:2]:
        copy.wait()
    slots = [out_slot[0, m] for m in range(n_move)]
    pages = [table[half, slot] for slot in slots]

    def fetch(index, moved, kept, arrived, buf, sem):
        stays = index >= 0
        for m in range(n_move):
            stays = stays & (index != moved[m])

            @pl.when(index == moved[m])
            def _(m=m):
                pltpu.make_async_copy(arrived.at[m], buf.at[index], sem).start()

        @pl.when(stays)
        def _():
            pltpu.make_async_copy(kept.at[index], buf.at[index], sem).start()

    for p in range(n_pool):
        fetch(jnp.int32(p), pages, pool, pages_in, page_buf, page_load.at[p])
    for r in range(n_req):
        fetch(jnp.int32(r), slots, mem, mem_in, mem_buf, mem_load.at[r])
    outs = []
    for p in range(n_pool):
        pltpu.make_async_copy(pool.at[p], page_buf.at[p], page_load.at[p]).wait()
        outs.append(pltpu.make_async_copy(page_buf.at[p], pool_out.at[p], page_sem.at[p]))
        outs[-1].start()
    for r in range(n_req):
        pltpu.make_async_copy(mem.at[r], mem_buf.at[r], mem_load.at[r]).wait()
        outs.append(pltpu.make_async_copy(mem_buf.at[r], mem_out.at[r], mem_sem.at[r]))
        outs[-1].start()
    smalls[2].wait()
    for copy in outs:
        copy.wait()


def body(
    n_rep, n_tp, tokens, lengths, prompt_group, span_close, out_slot, move_dest, page_table,
    cache_pool, prefix_cache, memory, norm_attn, norm_mlp, qkv_weight, out_weight, gate_weight,
    up_weight, down_weight, forget, write_rate,
):
    n_req, model_dim = tokens.shape
    n_pool, n_sect, page_len, width = cache_pool.shape
    half_dim, head_dim = memory.shape[2:]
    n_move = out_slot.shape[1]
    columns = qkv_weight.shape[1]
    block = math.gcd(columns, head_dim)
    row_len = n_move * model_dim // 128
    table = page_table[:, :, 0].T
    vmem = pl.BlockSpec(memory_space=pltpu.VMEM)
    hbm = pl.BlockSpec(memory_space=pltpu.HBM)
    if n_rep == 8:
        lead, moved_sems = (2, 5), (2, 4)
        page_piece = (n_move, n_sect, page_len // 2, width)
        mem_piece = (n_move, n_sect, half_dim // 2, head_dim)
        picks = (2,)
    else:
        lead, moved_sems = (n_rep,), (n_rep - 1,)
        page_piece = (n_move, n_sect, page_len, width)
        mem_piece = (n_move, n_sect, half_dim, head_dim)
        picks = ()
    page_pick = picks + page_piece if picks else (8, 128)
    mem_pick = picks + mem_piece if picks else (8, 128)
    V, dma = pltpu.VMEM, pltpu.SemaphoreType.DMA
    small = [lengths, prompt_group, span_close, out_slot, move_dest, table, forget, write_rate]
    gains = [norm_attn.reshape(1, model_dim), norm_mlp.reshape(1, model_dim)]
    whole = [tokens, qkv_weight, cache_pool, prefix_cache, memory, out_weight, gate_weight.T,
             up_weight.T, down_weight]
    rows, mem_after, mem_in, pages_in = pl.pallas_call(
        functools.partial(step_kernel, n_rep, n_tp),
        out_shape=(
            jax.ShapeDtypeStruct((n_req, model_dim), bf16),
            jax.ShapeDtypeStruct(memory.shape, f32),
            jax.ShapeDtypeStruct((n_move,) + memory.shape[1:], f32),
            jax.ShapeDtypeStruct((n_move,) + cache_pool.shape[1:], bf16),
        ),
        in_specs=[hbm] * 19,
        out_specs=(vmem, hbm, vmem, vmem),
        scratch_shapes=[pltpu.SMEM(a.shape, a.dtype) for a in small] + [
            V(a.shape, a.dtype) for a in gains + whole + [memory]
        ] + [
            V((n_tp * columns // block, n_req, block), bf16),
            V((n_rep, 8, 128), i32),
            V((n_sect + 1, n_req, 128), f32),
            V((n_sect + 1, n_req, 128), f32),
            V((n_tp, n_req, model_dim), bf16),
            V((n_tp, n_req, model_dim), bf16),
            V((n_rep, row_len, 128), bf16),
            V(lead + page_piece, bf16),
            V(lead + mem_piece, bf16),
            V(page_pick, bf16),
            V(mem_pick, bf16),
            dma((10,)), dma((9,)), dma,
            dma((n_tp - 1,)), dma((n_tp - 1,)),
            dma((n_rep - 1,)), dma((n_rep - 1,)),
            dma((2,)),
            dma((n_tp - 1,)), dma((n_tp - 1,)),
            dma((n_tp - 1,)), dma((n_tp - 1,)),
            dma((n_rep - 1,)), dma((n_rep - 1,)),
            dma(moved_sems), dma(moved_sems),
            dma(moved_sems), dma(moved_sems),
        ],
        compiler_params=pltpu.CompilerParams(
            collective_id=0, has_side_effects=True, vmem_limit_bytes=VMEM_BYTES
        ),
        name="step",
    )(*small, *gains, *whole)
    return pl.pallas_call(
        place_kernel,
        out_shape=(
            jax.ShapeDtypeStruct(rows.shape, bf16),
            jax.ShapeDtypeStruct(cache_pool.shape, bf16),
            jax.ShapeDtypeStruct(memory.shape, f32),
        ),
        in_specs=[hbm] * 7,
        out_specs=(vmem, hbm, hbm),
        scratch_shapes=[
            pltpu.SMEM(table.shape, i32), pltpu.SMEM(out_slot.shape, i32),
            V(cache_pool.shape, bf16), V(memory.shape, f32),
            dma((3,)), dma((n_pool,)), dma((n_req,)), dma((n_pool,)), dma((n_req,)),
        ],
        compiler_params=pltpu.CompilerParams(vmem_limit_bytes=VMEM_BYTES),
        name="place",
    )(table, out_slot, rows, cache_pool, pages_in, mem_after, mem_in)


def solution(mesh):
    row = P("rep", None)
    grid = P("rep", "tp", None, None)
    placed = (
        row, P("rep"), P("rep"), P("rep"), row, row, P("rep", None, None), grid,
        P(None, "tp", None, None), grid, P(), P(), P(None, "tp"), P("tp", None), P(None, "tp"),
        P(None, "tp"), P("tp", None), P(), P(),
    )

    def run(*args):
        rows, pool, mem = body(mesh.shape["rep"], mesh.shape["tp"], *args)
        return rows, mem, pool

    return jax.shard_map(
        run, mesh=mesh, in_specs=placed, out_specs=(row, grid, grid), check_vma=False
    )
```

```python
import functools
import math

import jax
import jax.numpy as jnp
from jax import lax
from jax.experimental import pallas as pl
from jax.experimental.pallas import tpu as pltpu
from jax.sharding import PartitionSpec as P

MESH = pl.DeviceIdType.MESH
f32, bf16, i32 = jnp.float32, jnp.bfloat16, jnp.int32
LOW = -1e30
VMEM_BYTES = 64 * 1024 * 1024


def split2(x):
    hi = x.astype(bf16)
    lo = (x - hi.astype(f32)).astype(bf16)
    return hi, lo


def dot_t(a, b):
    return lax.dot_general(a, b, (((1,), (1,)), ((), ())), preferred_element_type=f32)


def rms_scale(values, gain_vec):
    return values * lax.rsqrt(jnp.mean(values * values, axis=-1, keepdims=True) + 1e-05) * gain_vec


def unit_rows(values):
    return values * lax.rsqrt(jnp.sum(values * values, axis=-1, keepdims=True) + 1e-06)


def column(ref_values, count):
    rows = lax.broadcasted_iota(i32, (count, 1), 0)
    out = jnp.zeros((count, 1), i32)
    for r in range(count):
        out = jnp.where(rows == r, ref_values(r), out)
    return out


def step_kernel(
    n_rep, n_tp,
    lengths_hbm, group_hbm, span_hbm, out_slot_hbm, move_dest_hbm, table_hbm, forget_hbm,
    rate_hbm, norm_attn_hbm, norm_mlp_hbm, tokens_hbm, qkvw_hbm, pool_hbm, prefix_hbm, mem_hbm,
    outw_hbm, gatew_hbm, upw_hbm, downw_hbm,
    rows_out, mem_after, mem_in, pages_in,
    lengths, group, span, out_slot, move_dest, table, forget, rate,
    norm_attn, norm_mlp, tokens, qkvw, pool, prefix, mem, outw, gatew, upw, downw, mem_new,
    qbuf, dtab, part_send, part_recv, ar_one, ar_two, row_buf, held_page, held_mem,
    pick_page, pick_mem,
    dests, dest_sem, small_sem, load_sem, out_sem, q_send, q_recv, d_send, d_recv, part_sem, one_send, one_recv,
    two_send, two_recv, row_send, row_recv, page_send, page_recv, mem_send, mem_recv,
):
    n_req, model_dim = tokens.shape
    n_pool, n_sect, page_len, width = pool.shape
    head_dim = width // 2
    n_group, _, pre_len, _ = prefix.shape
    half_dim = mem.shape[2]
    n_head = model_dim // head_dim
    n_move = out_slot.shape[1]
    n_block, _, block = qbuf.shape
    own_blocks = n_block // n_tp
    per_head = head_dim // block
    routed = n_rep == 8
    scale = head_dim ** (-0.5)
    rep = lax.axis_index("rep")
    tp = lax.axis_index("tp")
    half = (tp * n_sect) // n_head

    def rep_flip(bits):
        return rep + bits * (1 - 2 * (lax.rem(lax.div(rep, bits), 2)))

    smalls = []
    for i, (src, dst) in enumerate([
        (norm_attn_hbm, norm_attn), (move_dest_hbm, move_dest), (out_slot_hbm, out_slot),
        (table_hbm, table), (lengths_hbm, lengths), (group_hbm, group), (span_hbm, span),
        (forget_hbm, forget), (rate_hbm, rate), (norm_mlp_hbm, norm_mlp),
    ]):
        copy = pltpu.make_async_copy(src, dst, small_sem.at[i])
        copy.start()
        smalls.append(copy)
    loads = []
    for i, (src, dst) in enumerate([
        (tokens_hbm, tokens), (qkvw_hbm, qkvw), (pool_hbm, pool), (prefix_hbm, prefix),
        (mem_hbm, mem), (outw_hbm, outw), (gatew_hbm, gatew), (upw_hbm, upw), (downw_hbm, downw),
    ]):
        loads.append(pltpu.make_async_copy(src, dst, load_sem.at[i]))
    for copy in loads[:2]:
        copy.start()

    barrier = pltpu.get_barrier_semaphore()
    for o in range(1, n_tp):
        pl.semaphore_signal(
            barrier, inc=1, device_id=(rep, lax.rem(tp + o, n_tp)), device_id_type=MESH
        )
    for o in range(1, n_rep):
        pl.semaphore_signal(
            barrier, inc=1, device_id=(lax.rem(rep + o, n_rep), tp), device_id_type=MESH
        )

    def tp_gather(buf_own, send, recv):
        copies = []
        for o in range(1, n_tp):
            copy = pltpu.make_async_remote_copy(
                src_ref=buf_own, dst_ref=buf_own, send_sem=send.at[o - 1], recv_sem=recv.at[o - 1],
                device_id=(rep, lax.rem(tp + o, n_tp)), device_id_type=MESH,
            )
            copy.start()
            copies.append(copy)
        return copies

    def rep_gather(buf_own, send, recv):
        copies = []
        for o in range(1, n_rep):
            copy = pltpu.make_async_remote_copy(
                src_ref=buf_own, dst_ref=buf_own, send_sem=send.at[o - 1], recv_sem=recv.at[o - 1],
                device_id=(lax.rem(rep + o, n_rep), tp), device_id_type=MESH,
            )
            copy.start()
            copies.append(copy)
        return copies

    def wait_all(copies):
        for copy in copies:
            copy.wait()

    wait_all(smalls)
    loads[0].wait()
    residual = tokens[...].astype(f32)
    normed = rms_scale(residual, norm_attn[...]).astype(bf16)
    lane = lax.broadcasted_iota(i32, (8, 128), 1)
    tags = jnp.zeros((8, 128), i32)
    for m in range(n_move):
        tags = jnp.where(lane == m, move_dest[0, m], tags)
    dtab[rep] = tags
    loads[1].wait()
    for copy in loads[2:5]:
        copy.start()
    qkv = jnp.dot(normed, qkvw[...], preferred_element_type=f32).astype(bf16)
    for b in range(own_blocks):
        qbuf[tp * own_blocks + b] = qkv[:, b * block:(b + 1) * block]

    pl.semaphore_wait(barrier, n_tp + n_rep - 2)
    q_copies = tp_gather(qbuf.at[pl.ds(tp * own_blocks, own_blocks)], q_send, q_recv)
    d_copies = rep_gather(dtab.at[rep], d_send, d_recv)

    def push(src, dst, send, recv, peer):
        copy = pltpu.make_async_remote_copy(
            src_ref=src, dst_ref=dst, send_sem=send, recv_sem=recv,
            device_id=(peer, tp), device_id_type=MESH,
        )
        copy.start()
        return copy

    first_bits, last_bits = (2, 4), (4, 2)

    def route_begin(held, send, recv):
        if not routed:
            return rep_gather(held.at[rep], send, recv)
        copies = []
        for k in range(2):
            copies.append(push(held.at[k, 0], held.at[k, 2], send.at[k, 0], recv.at[k, 0],
                               rep_flip(first_bits[k])))
        for k in range(2):
            copies.append(push(held.at[k, 0], held.at[k, 1], send.at[k, 1], recv.at[k, 1],
                               rep_flip(1)))
        return copies

    def route_forward(copies, held, send, recv):
        if not routed:
            return
        for k in range(2):
            copies[k].wait_recv()
            copies.append(push(held.at[k, 2], held.at[k, 3], send.at[k, 2], recv.at[k, 2],
                               rep_flip(1)))

    def dest_of(r, m):
        return dests[r, 0, m]

    def slot_rep(k, j):
        there = rep if j < 2 else rep_flip(first_bits[k])
        if j % 2:
            there = there + 1 - 2 * lax.rem(there, 2)
        return there

    def choose(held, k, m, s, wanted):
        out = held[k, 0, m, s].astype(f32)
        for j in range(1, 4):
            out = jnp.where(dest_of(slot_rep(k, j), m) == wanted, held[k, j, m, s].astype(f32), out)
        return out

    def route_last(copies, held, pick, send, recv):
        if not routed:
            return
        for copy in copies[2:6]:
            copy.wait_recv()
        for k in range(2):
            peer = rep_flip(last_bits[k])
            for m in range(n_move):
                for s in range(n_sect):
                    pick[k, m, s] = choose(held, k, m, s, peer).astype(bf16)
            copies.append(push(pick.at[k], held.at[k, 4], send.at[k, 3], recv.at[k, 3], peer))

    def route_end(copies, held, out_ref):
        if not routed:
            wait_all(copies)
            for m in range(n_move):
                for s in range(n_sect):
                    def body(r, acc):
                        return jnp.where(dest_of(r, m) == rep, held[r, m, s].astype(f32), acc)
                    out_ref[m, s] = lax.fori_loop(
                        0, n_rep, body, jnp.zeros(out_ref.shape[2:], f32)
                    ).astype(out_ref.dtype)
            return
        for copy in copies[6:8]:
            copy.wait_recv()
        for copy in copies:
            copy.wait_send()
        rows = held.shape[4]
        for k in range(2):
            for m in range(n_move):
                for s in range(n_sect):
                    out = held[k, 4, m, s].astype(f32)
                    for j in range(4):
                        out = jnp.where(dest_of(slot_rep(k, j), m) == rep,
                                        held[k, j, m, s].astype(f32), out)
                    out_ref[m, s, pl.ds(k * rows, rows)] = out.astype(out_ref.dtype)

    loads[2].wait()
    for copy in loads[5:]:
        copy.start()
    for m in range(n_move):
        page = table[half, out_slot[0, m]]
        for s in range(n_sect):
            leaving = pool[page, s]
            if routed:
                cut = page_len // 2
                held_page[0, 0, m, s] = leaving[:cut]
                held_page[1, 0, m, s] = leaving[cut:]
            else:
                held_page[rep, m, s] = leaving
    page_copies = route_begin(held_page, page_send, page_recv)

    page_col = column(lambda r: table[half, r], n_req)
    length_col = column(lambda r: lengths[r], n_req)
    group_col = column(lambda r: group[r], n_req)
    span_col = column(lambda r: span[r], n_req)
    keys_at = lax.broadcasted_iota(i32, (n_req, n_pool * page_len), 1)
    page_from = page_col * page_len
    live_count = jnp.minimum(length_col - half * page_len, page_len)
    live_pool = (keys_at >= page_from) & (keys_at < page_from + live_count)
    pre_at = lax.broadcasted_iota(i32, (n_req, n_group * pre_len), 1)
    live_pre = (pre_at >= group_col * pre_len) & (pre_at < (group_col + 1) * pre_len)
    mem_at = lax.broadcasted_iota(i32, (n_req, n_req * half_dim), 1)
    mem_from = lax.broadcasted_iota(i32, (n_req, n_req * half_dim), 0) * half_dim
    mine = (mem_at >= mem_from) & (mem_at < mem_from + half_dim)
    writes = mine & (span_col == 1)
    loads[3].wait()
    wait_all(q_copies)

    def head_rows(base, s):
        head = lax.rem(tp * n_sect + s, n_head)
        parts = [qbuf[base * n_head * per_head + head * per_head + j] for j in range(per_head)]
        return parts[0] if per_head == 1 else jnp.concatenate(parts, axis=1)

    queries = [head_rows(0, s) for s in range(n_sect)]
    new_keys = [head_rows(1, s).astype(f32) for s in range(n_sect)]
    new_values = [head_rows(2, s).astype(f32) for s in range(n_sect)]
    wide = lax.broadcasted_iota(i32, (n_req, 128), 1)
    stats = jnp.zeros((n_req, 128), f32)
    tops, denoms, accs, others = [], [], [], []

    def own_half(x):
        return jnp.where(half == 0, x[:, :half_dim], x[:, half_dim:])

    for s in range(n_sect):
        q = queries[s]
        k_pool = pool[:, s, :, :head_dim].reshape(n_pool * page_len, head_dim)
        v_pool = pool[:, s, :, head_dim:].reshape(n_pool * page_len, head_dim)
        k_pre = prefix[:, s, :, :head_dim].reshape(n_group * pre_len, head_dim)
        v_pre = prefix[:, s, :, head_dim:].reshape(n_group * pre_len, head_dim)
        s_pool = jnp.where(live_pool, dot_t(q, k_pool) * scale, LOW)
        s_pre = jnp.where(live_pre, dot_t(q, k_pre) * scale, LOW)
        own = jnp.sum(q.astype(f32) * new_keys[s], axis=-1, keepdims=True) * scale
        own = jnp.where(half == 0, own, LOW)
        top = jnp.maximum(jnp.max(s_pool, axis=-1, keepdims=True),
                          jnp.max(s_pre, axis=-1, keepdims=True))
        top = jnp.maximum(top, own)
        w_pool = jnp.exp(s_pool - top)
        w_pre = jnp.exp(s_pre - top)
        w_own = jnp.exp(own - top)
        denom = (jnp.sum(w_pool, axis=-1, keepdims=True) + jnp.sum(w_pre, axis=-1, keepdims=True)
                 + w_own)
        both = jnp.dot(jnp.concatenate(split2(w_pool), axis=0), v_pool, preferred_element_type=f32)
        both = both + jnp.dot(
            jnp.concatenate(split2(w_pre), axis=0), v_pre, preferred_element_type=f32
        )
        acc = both[:n_req] + both[n_req:] + w_own * new_values[s]
        stats = jnp.where(wide == s, top, stats)
        stats = jnp.where(wide == 64 + s, denom, stats)
        tops.append(top)
        denoms.append(denom)
        accs.append(own_half(acc))
        others.append(jnp.where(half == 0, acc[:, half_dim:], acc[:, :half_dim]))
    if n_sect % 2:
        others.append(jnp.zeros((n_req, half_dim), f32))
    n_pair = len(others) // 2
    for s in range(n_pair):
        part_send[s] = jnp.concatenate(others[2 * s:2 * s + 2], axis=1)
    part_send[n_pair] = stats
    partner = lax.rem(tp + n_tp // 2, n_tp)
    part_copy = pltpu.make_async_remote_copy(
        src_ref=part_send, dst_ref=part_recv, send_sem=part_sem.at[0], recv_sem=part_sem.at[1],
        device_id=(rep, partner), device_id_type=MESH,
    )
    part_copy.start()

    loads[4].wait()
    recalls, predicts, units = [], [], []

    for s in range(n_sect):
        q_hi, q_lo = split2(unit_rows(queries[s].astype(f32)))
        k_hi, k_lo = split2(unit_rows(new_keys[s]))
        m_hi, m_lo = split2(mem[:, s].reshape(n_req * half_dim, head_dim))
        by_hi = dot_t(jnp.concatenate([q_hi, k_hi, q_lo, k_lo], axis=0), m_hi)
        by_lo = dot_t(jnp.concatenate([q_hi, k_hi], axis=0), m_lo)
        seen = by_hi[:2 * n_req] + by_hi[2 * n_req:] + by_lo
        recalled = jnp.where(mine, seen[:n_req], 0.0)
        fold = recalled[:, :128]
        for c in range(1, n_req * half_dim // 128):
            fold = fold + recalled[:, c * 128:(c + 1) * 128]
        recalls.append(fold[:, :half_dim] + fold[:, half_dim:])
        predicts.append(seen[n_req:])
        units.append((k_hi, k_lo))
    wait_all(d_copies)
    dest_copy = pltpu.make_async_copy(dtab, dests, dest_sem)
    dest_copy.start()
    route_forward(page_copies, held_page, page_send, page_recv)

    part_copy.wait()
    theirs = part_recv[n_pair]
    mixed = []
    for s in range(n_sect):
        top_b = jnp.sum(jnp.where(wide == s, theirs, 0.0), axis=-1, keepdims=True)
        den_b = jnp.sum(jnp.where(wide == 64 + s, theirs, 0.0), axis=-1, keepdims=True)
        top = jnp.maximum(tops[s], top_b)
        w_a, w_b = jnp.exp(tops[s] - top), jnp.exp(top_b - top)
        came = part_recv[s // 2][:, (s % 2) * half_dim:(s % 2 + 1) * half_dim]
        total = accs[s] * w_a + came * w_b
        attended = total / (denoms[s] * w_a + den_b * w_b)
        mixed.append(attended + recalls[s])
    mixed = mixed[0] if n_sect == 1 else jnp.concatenate(mixed, axis=1)
    loads[5].wait()
    ar_one[tp] = jnp.dot(mixed.astype(bf16), outw[...], preferred_element_type=f32).astype(bf16)
    one_copies = tp_gather(ar_one.at[tp], one_send, one_recv)
    dest_copy.wait()
    route_last(page_copies, held_page, pick_page, page_send, page_recv)

    for s in range(n_sect):
        head = lax.rem(tp * n_sect + s, n_head)
        k_hi, k_lo = units[s]
        value = jnp.concatenate([own_half(new_values[s])] * n_req, axis=1)
        miss = jnp.where(writes, rate[head] * (value - predicts[s]), 0.0)
        miss_hi = miss.astype(bf16).astype(f32)
        stack = jnp.concatenate([miss_hi, miss - miss_hi, miss_hi], axis=0)
        grow = jnp.dot(
            jnp.transpose(stack).astype(bf16), jnp.concatenate([k_hi, k_hi, k_lo], axis=0),
            preferred_element_type=f32,
        )
        keep = forget[head]
        for r in range(n_req):
            kept = jnp.where(span[r] == 1, keep, 1.0)
            mem_new[r, s] = kept * mem[r, s] + grow[r * half_dim:(r + 1) * half_dim]
    mem_copy = pltpu.make_async_copy(mem_new, mem_after, out_sem)
    mem_copy.start()
    for m in range(n_move):
        for s in range(n_sect):
            leaving = mem_new[out_slot[0, m], s].astype(bf16)
            if routed:
                cut = half_dim // 2
                held_mem[0, 0, m, s] = leaving[:cut]
                held_mem[1, 0, m, s] = leaving[cut:]
            else:
                held_mem[rep, m, s] = leaving
    mem_copies = route_begin(held_mem, mem_send, mem_recv)
    wait_all(one_copies)
    hidden = residual
    for t in range(n_tp):
        hidden = hidden + ar_one[t].astype(f32)
    normed = rms_scale(hidden, norm_mlp[...]).astype(bf16)
    loads[6].wait()
    gate = dot_t(normed, gatew[...])
    loads[7].wait()
    up = dot_t(normed, upw[...])
    activated = (gate * jax.nn.sigmoid(gate) * up).astype(bf16)
    loads[8].wait()
    ar_two[tp] = jnp.dot(activated, downw[...], preferred_element_type=f32).astype(bf16)
    two_copies = tp_gather(ar_two.at[tp], two_send, two_recv)
    route_forward(mem_copies, held_mem, mem_send, mem_recv)
    wait_all(two_copies)
    total = ar_two[0].astype(f32)
    for t in range(1, n_tp):
        total = total + ar_two[t].astype(f32)
    rows = (hidden + total).astype(bf16)

    n_piece = model_dim // 128
    row_len = row_buf.shape[1]
    to_buf = lax.broadcasted_iota(i32, (row_len, n_req), 0)
    from_slot = lax.broadcasted_iota(i32, (row_len, n_req), 1)
    packed = jnp.zeros((row_len, 128), f32)
    for c in range(n_piece):
        hot = jnp.zeros((row_len, n_req), f32)
        for m in range(n_move):
            hot = jnp.where((to_buf == c * n_move + m) & (from_slot == out_slot[0, m]), 1.0, hot)
        packed = packed + jnp.dot(
            hot.astype(bf16), rows[:, c * 128:(c + 1) * 128], preferred_element_type=f32
        )
    row_buf[rep] = packed.astype(bf16)
    row_copies = rep_gather(row_buf.at[rep], row_send, row_recv)
    route_last(mem_copies, held_mem, pick_mem, mem_send, mem_recv)
    route_end(page_copies, held_page, pages_in)
    wait_all(row_copies)
    arrived = row_buf[...].reshape(n_rep * row_len, 128)
    slot_at = lax.broadcasted_iota(i32, (n_req, row_len), 0)
    buf_at = lax.broadcasted_iota(i32, (n_req, row_len), 1)
    slot_col = lax.broadcasted_iota(i32, (n_req, 1), 0)
    staying = jnp.ones((n_req, 1), jnp.bool_)
    for m in range(n_move):
        staying = staying & (slot_col != out_slot[0, m])
    chosen = jnp.zeros((row_len, 128), f32)
    buf_move = lax.broadcasted_iota(i32, (row_len, 128), 0) % n_move
    for r in range(n_rep):
        hit = jnp.zeros((row_len, 128), i32)
        for m in range(n_move):
            hit = jnp.where((buf_move == m) & (dest_of(r, m) == rep), 1, hit)
        chosen = jnp.where(hit == 1, row_buf[r].astype(f32), chosen)
    chosen = chosen.astype(bf16)
    for c in range(n_piece):
        hot = jnp.zeros((n_req, row_len), f32)
        for m in range(n_move):
            hot = jnp.where((buf_at == c * n_move + m) & (slot_at == out_slot[0, m]), 1.0, hot)
        came = jnp.dot(hot.astype(bf16), chosen, preferred_element_type=f32)
        kept = rows[:, c * 128:(c + 1) * 128].astype(f32)
        rows_out[:, c * 128:(c + 1) * 128] = jnp.where(staying, kept, came).astype(bf16)
    route_end(mem_copies, held_mem, mem_in)
    mem_copy.wait()


def place_kernel(
    table_hbm, out_slot_hbm, rows_hbm, pool, pages_in, mem, mem_in, rows_out, pool_out, mem_out,
    table, out_slot, page_buf, mem_buf, small_sem, page_load, mem_load, page_sem, mem_sem,
):
    smalls = [
        pltpu.make_async_copy(table_hbm, table, small_sem.at[0]),
        pltpu.make_async_copy(out_slot_hbm, out_slot, small_sem.at[1]),
        pltpu.make_async_copy(rows_hbm, rows_out, small_sem.at[2]),
    ]
    for copy in smalls:
        copy.start()
    n_pool, n_sect = pool.shape[0], pool.shape[1]
    n_req = mem.shape[0]
    n_head = rows_hbm.shape[1] // mem.shape[3]
    n_move = out_slot.shape[1]
    half = (lax.axis_index("tp") * n_sect) // n_head
    page_loads, mem_loads = [], []
    for m in range(n_move):
        page_loads.append(pltpu.make_async_copy(
            pages_in.at[m], page_buf.at[n_pool + m], page_load.at[n_pool + m]))
        mem_loads.append(pltpu.make_async_copy(
            mem_in.at[m], mem_buf.at[n_req + m], mem_load.at[n_req + m]))
    for p in range(n_pool):
        page_loads.append(pltpu.make_async_copy(pool.at[p], page_buf.at[p], page_load.at[p]))
    for r in range(n_req):
        mem_loads.append(pltpu.make_async_copy(mem.at[r], mem_buf.at[r], mem_load.at[r]))
    for copy in page_loads + mem_loads:
        copy.start()
    for copy in smalls[:2]:
        copy.wait()
    slots = [out_slot[0, m] for m in range(n_move)]
    pages = [table[half, slot] for slot in slots]
    outs = []

    def store(index, count, moved, buf, out, sem):
        source = jnp.int32(index)
        for m in range(n_move):
            source = jnp.where(moved[m] == index, count + m, source)
        copy = pltpu.make_async_copy(buf.at[source], out.at[index], sem.at[index])
        copy.start()
        outs.append(copy)

    for copy in page_loads[:n_move]:
        copy.wait()
    for p in range(n_pool):
        page_loads[n_move + p].wait()
        store(p, n_pool, pages, page_buf, pool_out, page_sem)
    for copy in mem_loads[:n_move]:
        copy.wait()
    for r in range(n_req):
        mem_loads[n_move + r].wait()
        store(r, n_req, slots, mem_buf, mem_out, mem_sem)
    smalls[2].wait()
    for copy in outs:
        copy.wait()


def body(
    n_rep, n_tp, tokens, lengths, prompt_group, span_close, out_slot, move_dest, page_table,
    cache_pool, prefix_cache, memory, norm_attn, norm_mlp, qkv_weight, out_weight, gate_weight,
    up_weight, down_weight, forget, write_rate,
):
    n_req, model_dim = tokens.shape
    n_pool, n_sect, page_len, width = cache_pool.shape
    half_dim, head_dim = memory.shape[2:]
    n_move = out_slot.shape[1]
    columns = qkv_weight.shape[1]
    block = math.gcd(columns, head_dim)
    row_len = n_move * model_dim // 128
    table = page_table[:, :, 0].T
    vmem = pl.BlockSpec(memory_space=pltpu.VMEM)
    hbm = pl.BlockSpec(memory_space=pltpu.HBM)
    if n_rep == 8:
        lead, moved_sems = (2, 5), (2, 4)
        page_piece = (n_move, n_sect, page_len // 2, width)
        mem_piece = (n_move, n_sect, half_dim // 2, head_dim)
        picks = (2,)
    else:
        lead, moved_sems = (n_rep,), (n_rep - 1,)
        page_piece = (n_move, n_sect, page_len, width)
        mem_piece = (n_move, n_sect, half_dim, head_dim)
        picks = ()
    page_pick = picks + page_piece if picks else (8, 128)
    mem_pick = picks + mem_piece if picks else (8, 128)
    V, dma = pltpu.VMEM, pltpu.SemaphoreType.DMA
    small = [lengths, prompt_group, span_close, out_slot, move_dest, table, forget, write_rate]
    gains = [norm_attn.reshape(1, model_dim), norm_mlp.reshape(1, model_dim)]
    whole = [tokens, qkv_weight, cache_pool, prefix_cache, memory, out_weight, gate_weight.T,
             up_weight.T, down_weight]
    rows, mem_after, mem_in, pages_in = pl.pallas_call(
        functools.partial(step_kernel, n_rep, n_tp),
        out_shape=(
            jax.ShapeDtypeStruct((n_req, model_dim), bf16),
            jax.ShapeDtypeStruct(memory.shape, f32),
            jax.ShapeDtypeStruct((n_move,) + memory.shape[1:], f32),
            jax.ShapeDtypeStruct((n_move,) + cache_pool.shape[1:], bf16),
        ),
        in_specs=[hbm] * 19,
        out_specs=(vmem, hbm, vmem, vmem),
        scratch_shapes=[pltpu.SMEM(a.shape, a.dtype) for a in small] + [
            V(a.shape, a.dtype) for a in gains + whole + [memory]
        ] + [
            V((n_tp * columns // block, n_req, block), bf16),
            V((n_rep, 8, 128), i32),
            V(((n_sect + 1) // 2 + 1, n_req, 128), f32),
            V(((n_sect + 1) // 2 + 1, n_req, 128), f32),
            V((n_tp, n_req, model_dim), bf16),
            V((n_tp, n_req, model_dim), bf16),
            V((n_rep, row_len, 128), bf16),
            V(lead + page_piece, bf16),
            V(lead + mem_piece, bf16),
            V(page_pick, bf16),
            V(mem_pick, bf16),
            pltpu.SMEM((n_rep, 8, 128), i32), dma,
            dma((10,)), dma((9,)), dma,
            dma((n_tp - 1,)), dma((n_tp - 1,)),
            dma((n_rep - 1,)), dma((n_rep - 1,)),
            dma((2,)),
            dma((n_tp - 1,)), dma((n_tp - 1,)),
            dma((n_tp - 1,)), dma((n_tp - 1,)),
            dma((n_rep - 1,)), dma((n_rep - 1,)),
            dma(moved_sems), dma(moved_sems),
            dma(moved_sems), dma(moved_sems),
        ],
        compiler_params=pltpu.CompilerParams(
            collective_id=0, has_side_effects=True, vmem_limit_bytes=VMEM_BYTES
        ),
        name="step",
    )(*small, *gains, *whole)
    return pl.pallas_call(
        place_kernel,
        out_shape=(
            jax.ShapeDtypeStruct(rows.shape, bf16),
            jax.ShapeDtypeStruct(cache_pool.shape, bf16),
            jax.ShapeDtypeStruct(memory.shape, f32),
        ),
        in_specs=[hbm] * 7,
        out_specs=(vmem, hbm, hbm),
        scratch_shapes=[
            pltpu.SMEM(table.shape, i32), pltpu.SMEM(out_slot.shape, i32),
            V((n_pool + n_move,) + cache_pool.shape[1:], bf16),
            V((n_req + n_move,) + memory.shape[1:], f32),
            dma((3,)), dma((n_pool + n_move,)), dma((n_req + n_move,)), dma((n_pool,)),
            dma((n_req,)),
        ],
        compiler_params=pltpu.CompilerParams(vmem_limit_bytes=VMEM_BYTES),
        name="place",
    )(table, out_slot, rows, cache_pool, pages_in, mem_after, mem_in)


def solution(mesh):
    row = P("rep", None)
    grid = P("rep", "tp", None, None)
    placed = (
        row, P("rep"), P("rep"), P("rep"), row, row, P("rep", None, None), grid,
        P(None, "tp", None, None), grid, P(), P(), P(None, "tp"), P("tp", None), P(None, "tp"),
        P(None, "tp"), P("tp", None), P(), P(),
    )

    def run(*args):
        rows, pool, mem = body(mesh.shape["rep"], mesh.shape["tp"], *args)
        return rows, mem, pool

    return jax.shard_map(
        run, mesh=mesh, in_specs=placed, out_specs=(row, grid, grid), check_vma=False
    )
```
